128 devices in a mesh: atoms: 16 (over y_hi, z, core), kvec: 8 (over y_lo, x).
Axes of the slice: x: 4, y: 4 (y_hi: 2, y_lo: 2; y = y_hi * 2 + y_lo), z: 4, core: 2. Of those that a mesh axis runs over, the one named last changes fastest.
Arguments:
- positions: float32 [3, 32768], P(None, ('atoms', 'kvec')), may hold values from 0 to 8
- features: bfloat16 [32768, 128], P(('atoms', 'kvec')), may hold values from -6 to 6
- atom_mask: int32 [32768], P(('atoms', 'kvec')), may hold values 0 or 1
- neighbours: int32 [256, 12], P(('atoms', 'kvec')), may hold values from 0 to 255, as said below
- lattice: int32 [3, 12288], P(None, 'kvec'), may hold values from -15 to 15, as said below
- pair_weight: bfloat16 [1024, 128], replicated, may hold values from -0.1875 to 0.1875
- kfilter: float32 [8, 128], replicated, may hold values from -4 to 4
- norm_gain: float32 [128], replicated, may hold values from 0.25 to 1.75
- w_in: bfloat16 [128, 512], replicated, may hold values from -0.5 to 0.5
- w_out: bfloat16 [512, 128], replicated, may hold values from -0.25 to 0.25
Outputs:
- updated: bfloat16 [32768, 128], P(('atoms', 'kvec'))
The draws below stay inside these ranges and needn't reach their ends.
Inputs may be any that keep to these rules, and one draw needn't show every extreme that they name: `neighbours`: group of a block = its id // 16. The 12 ids of a block are different and each lies in the block's group, the group below or the group above it, cyclically over the 16 groups. `lattice`: the 12288 wavevectors are distinct, none is zero, and no two are negatives of each other.
All inputs are finite; a program needn't handle non-finite values. No bound on the sum of `atom_mask` on one device may be relied on, other than what follows from the above.
Results may differ from the reference program's by a relative error of at most 0.017.
Values may be sent and summed in bfloat16 or wider, within the bound.
A program may use at most 64 MiB of HBM per device.

```python
import math
import jax
import jax.numpy as jnp
from jax import lax

C = 128
HID = 512
KW = 12288
KB = 8
KQ = 8
BLOCK_ATOMS = 128
NS = 12
ATOMS = 32768
NBLK = 256
GROUP_BLK = 16


def draw_neighbours(key, part):
    feature_width = 3 * GROUP_BLK
    scores = jax.random.randint(key, (NBLK, feature_width), 0, 1 << 16)
    scores = scores * feature_width + jnp.arange(feature_width, dtype=jnp.int32)[None, :]
    _, picked = lax.top_k(scores, NS)
    group = jnp.arange(NBLK, dtype=jnp.int32) // GROUP_BLK
    atom_identifiers = ((group[:, None] - 1) * GROUP_BLK + picked.astype(jnp.int32)) % NBLK
    return atom_identifiers.astype(jnp.int32)


def draw_lattice(key, part):
    order = jax.random.permutation(jax.random.fold_in(key, 7), 14895).astype(jnp.int32)
    code = order[:KW] + 14896
    first = code // 961 - 15
    second = code // 31 % 31 - 15
    third = code % 31 - 15
    return jnp.stack([first, second, third], axis=0).astype(jnp.int32)


def plant(array, rng, low, top_value):
    index_at = [jax.random.randint(jax.random.fold_in(rng, axis), (), 0, length) for axis, length in enumerate(array.shape)]
    widest = array.shape.index(max(array.shape))
    next_to = index_at[:widest] + [(index_at[widest] + 1) % array.shape[widest]] + index_at[widest + 1:]
    return array.at[tuple(index_at)].set(low).at[tuple(next_to)].set(top_value)


def level_of(stream_key, dims, shards, least, largest):
    def one(dim, shards_of):
        steps = jax.random.uniform(jax.random.fold_in(jax.random.fold_in(stream_key, 6), dim), (shards_of,), jnp.float32, least / len(shards), largest / len(shards))
        return jnp.repeat(jnp.exp(steps), dims[dim] // shards_of).reshape((-1,) + (1,) * (len(dims) - dim - 1))

    loudness = one(*shards[0])
    for cut in shards[1:]:
        loudness = loudness * one(*cut)
    return loudness


def gaussian(rng, extent, spread, most, shards=(), kind=jnp.bfloat16):
    loudness = level_of(rng, extent, shards, -0.22, 0.18) if shards else 1.0
    array = jax.random.normal(rng, extent, jnp.float32) * spread * loudness
    return jnp.minimum(jnp.maximum(array, -most), most).astype(kind)


def setup_inputs(seed: int = 0) -> dict:
    arg_keys = jax.random.split(jax.random.key(seed), 11)
    positions = jnp.clip(8.0 * jax.random.uniform(arg_keys[0], (3, ATOMS), jnp.float32) ** level_of(arg_keys[0], (3, ATOMS), ((1, 128),), -0.2, 0.2), 0.0, 8.0)
    features = gaussian(arg_keys[1], (ATOMS, C), 1.0, 6.0, ((0, 128),))
    atom_mask = plant((jax.random.randint(arg_keys[2], (ATOMS,), 0, 8) < 7).astype(jnp.int32), jax.random.fold_in(arg_keys[2], 1), 0, 1)
    neighbours = draw_neighbours(jax.random.fold_in(arg_keys[10], 71), 0)
    lattice = draw_lattice(jax.random.fold_in(arg_keys[10], 71), 0)
    pair_weight = gaussian(arg_keys[5], (KB * C, C), (KB * C) ** -0.5, 0.1875)
    kfilter = gaussian(arg_keys[6], (KQ, C), 1.0, 4.0, (), jnp.float32)
    norm_gain = jnp.clip(1.0 + 0.15 * jax.random.normal(arg_keys[7], (C,), jnp.float32), 0.25, 1.75)
    w_in = gaussian(arg_keys[8], (C, HID), C ** -0.5, 0.5)
    w_out = gaussian(arg_keys[9], (HID, C), HID ** -0.5, 0.25)
    return {"positions": positions, "features": features, "atom_mask": atom_mask, "neighbours": neighbours, "lattice": lattice, "pair_weight": pair_weight, "kfilter": kfilter, "norm_gain": norm_gain, "w_in": w_in, "w_out": w_out}


def trig_tables(pos, wave):
    phase = pos[0][:, None] * wave[0][None, :] + pos[1][:, None] * wave[1][None, :] + pos[2][:, None] * wave[2][None, :]
    return (jnp.cos(phase).astype(jnp.bfloat16), jnp.sin(phase).astype(jnp.bfloat16))

def radial_filter(wave, kfilter):
    nbasis = kfilter.shape[0]
    kmag = jnp.sqrt(wave[0] * wave[0] + wave[1] * wave[1] + wave[2] * wave[2])
    centers = (jnp.arange(nbasis, dtype=jnp.float32) + 0.5) * (21.0 / nbasis)
    basis = jnp.exp(-0.5 * ((kmag[:, None] - centers[None, :]) / (21.0 / nbasis)) ** 2)
    return lax.optimization_barrier(jnp.sum(basis[:, :, None] * kfilter[None, :, :], axis=1))

def pair_block(own_pos, own_index, nearby_coordinates, nearby_feature_rows, nearby_atom_index, pair_weight, output_scale):
    feature_width = nearby_feature_rows.shape[1]
    nbasis = pair_weight.shape[0] // feature_width
    own_count = own_pos.shape[1]
    dist2 = (own_pos[0][:, None] - nearby_coordinates[0][None, :]) ** 2
    dist2 = dist2 + (own_pos[1][:, None] - nearby_coordinates[1][None, :]) ** 2
    dist2 = dist2 + (own_pos[2][:, None] - nearby_coordinates[2][None, :]) ** 2
    radius = jnp.sqrt(dist2)
    keep = (own_index[:, None] != nearby_atom_index[None, :]).astype(jnp.float32)
    env = keep * output_scale / (1.0 + (radius / 4.0) ** 2)
    centers = (jnp.arange(nbasis, dtype=jnp.float32) + 0.5) * (12.0 / nbasis)
    basis = jnp.exp(-0.5 * ((radius[None] - centers[:, None, None]) / (12.0 / nbasis)) ** 2) * env[None]
    basis = basis.astype(jnp.bfloat16).reshape(nbasis * own_count, radius.shape[1])
    summed = jnp.dot(basis, nearby_feature_rows, preferred_element_type=jnp.float32)
    summed = summed.reshape(nbasis, own_count, feature_width).transpose(1, 0, 2)
    summed = summed.reshape(own_count, nbasis * feature_width).astype(jnp.bfloat16)
    return jnp.dot(summed, pair_weight, preferred_element_type=jnp.float32)

def reference(positions, features, atom_mask, neighbours, lattice, pair_weight, kfilter, norm_gain, w_in, w_out):
    maskf = atom_mask.astype(jnp.float32)
    masked = (features.astype(jnp.float32) * maskf[:, None]).astype(jnp.bfloat16)
    nblk = ATOMS // BLOCK_ATOMS
    position_block_rows = positions.reshape(3, nblk, BLOCK_ATOMS)
    feature_block_rows = masked.reshape(nblk, BLOCK_ATOMS, C)
    output_scale = float(NS * BLOCK_ATOMS) ** (-0.5)
    block_offsets = jnp.arange(BLOCK_ATOMS, dtype=jnp.int32)

    def one_block(index):
        atom_identifiers = neighbours[index]
        nearby_coordinates = position_block_rows[:, atom_identifiers].reshape(3, NS * BLOCK_ATOMS)
        nearby_feature_rows = feature_block_rows[atom_identifiers].reshape(NS * BLOCK_ATOMS, C)
        nearby_atom_index = (atom_identifiers[:, None] * BLOCK_ATOMS + block_offsets[None, :]).reshape(NS * BLOCK_ATOMS)
        return pair_block(position_block_rows[:, index], index * BLOCK_ATOMS + block_offsets, nearby_coordinates, nearby_feature_rows, nearby_atom_index, pair_weight, output_scale)
    pair_msg = lax.map(one_block, jnp.arange(nblk, dtype=jnp.int32)).reshape(ATOMS, C)
    wave = lattice.astype(jnp.float32) * (2.0 * math.pi / 8.0)
    rows = 512 if ATOMS % 512 == 0 else ATOMS
    steps = ATOMS // rows

    def accumulate(carry, index):
        start = index * rows
        pos = lax.dynamic_slice_in_dim(positions, start, rows, 1)
        feat = lax.dynamic_slice_in_dim(masked, start, rows, 0)
        cosines, sines = trig_tables(pos, wave)
        part_c = jnp.dot(cosines.T, feat, preferred_element_type=jnp.float32)
        part_s = jnp.dot(sines.T, feat, preferred_element_type=jnp.float32)
        return ((carry[0] + part_c, carry[1] + part_s), None)
    zero = jnp.zeros((KW, C), jnp.float32)
    (factor_c, factor_s), _ = lax.scan(accumulate, (zero, zero), jnp.arange(steps, dtype=jnp.int32))
    kfilt = radial_filter(wave, kfilter) * float(ATOMS * KW) ** (-0.5)
    filt_c = (kfilt * factor_c).astype(jnp.bfloat16)
    filt_s = (kfilt * factor_s).astype(jnp.bfloat16)

    def inverse(index):
        pos = lax.dynamic_slice_in_dim(positions, index * rows, rows, 1)
        cosines, sines = trig_tables(pos, wave)
        return jnp.dot(cosines, filt_c, preferred_element_type=jnp.float32) + jnp.dot(sines, filt_s, preferred_element_type=jnp.float32)
    long_msg = lax.map(inverse, jnp.arange(steps, dtype=jnp.int32)).reshape(ATOMS, C)
    total = features.astype(jnp.float32) + pair_msg + long_msg
    normed = (total * lax.rsqrt(lax.optimization_barrier(jnp.mean(total * total, axis=-1, keepdims=True)) + 1e-06) * norm_gain).astype(jnp.bfloat16)
    hidden = jax.nn.silu(jnp.dot(normed, w_in, preferred_element_type=jnp.float32)).astype(jnp.bfloat16)
    return (total + jnp.dot(hidden, w_out, preferred_element_type=jnp.float32)).astype(jnp.bfloat16)
```

```python
import math

import jax
import jax.numpy as jnp
from jax import lax
from jax.experimental import pallas as pl
from jax.experimental.pallas import tpu as pltpu
from jax.sharding import PartitionSpec as P

MESH = pl.DeviceIdType.MESH
F32 = jnp.float32
BF16 = jnp.bfloat16
KW = 12288
BLK = 128
C = 128
KB = 8
KQ = 8
NS = 12
ATOMS = 32768
NT = (((1,), (1,)), ((), ()))

SIN = tuple((-1.0) ** i / math.factorial(2 * i + 1) for i in range(6))
COS = tuple((-1.0) ** i / math.factorial(2 * i) for i in range(7))


def poly(h2, coefs):
    total = h2 * coefs[-1] + coefs[-2]
    for c in coefs[-3::-1]:
        total = total * h2 + c
    return total


def sincos_turns(turns):
    h = (turns - jnp.floor(turns + 0.5)) * math.pi
    h2 = h * h
    s = h * poly(h2, SIN)
    c = poly(h2, COS)
    return 2.0 * s * c, 1.0 - 2.0 * s * s


def kernel(
    pos_ref, feat_ref, mask_ref, nb_ref, lat_ref, pw_ref, kfilter_ref, gain_ref, win_ref, wout_ref,
    out_ref,
    head, feats, tabs, ztab, zm, acc, pres, kft, pbuf, rbuf, gbuf, part, lown, sibs, sibin, lsend, lbuf,
    basis, near, summed, pair,
    g_hs, g_hr, g_fs, g_fr, s_hs, s_hr, s_fs, s_fr, h_s, h_r, x_hs, x_hr, x_fs, x_fr,
    r_s, r_r, a_s, a_r, b_s, b_r, l_s, l_r,
):
    a = lax.axis_index("atoms")
    k = lax.axis_index("kvec")
    core = lax.rem(a, 2)
    g = a // 2
    other = 1 - core
    sib = (g * 2 + other, k)

    def kpeer(d):
        return ((k // 4 + d // 4) % 2) * 4 + (k % 4 + d % 4) % 4

    def gpeer(d):
        return ((g // 4 + d // 4) % 2) * 4 + (g % 4 + d % 4) % 4

    halo_dev = (((g + jnp.where(core == 1, 1, 7)) % 8) * 2 + other, k)

    barrier = pltpu.get_barrier_semaphore()
    for d in range(1, 8):
        pl.semaphore_signal(barrier, inc=1, device_id=(a, kpeer(d)), device_id_type=MESH)
        pl.semaphore_signal(barrier, inc=1, device_id=(gpeer(d) * 2 + core, k), device_id_type=MESH)
    pl.semaphore_signal(barrier, inc=1, device_id=sib, device_id_type=MESH)
    pl.semaphore_signal(barrier, inc=1, device_id=halo_dev, device_id_type=MESH)

    def at_core(c, kk):
        return 16 + c * 16 + 2 * kk

    def at_halo(c, kk):
        return c * 48 + 2 * kk

    own = at_core(core, k)
    lat = lat_ref[:, pl.ds(pl.multiple_of(core * 768, 128), 768)]
    nx, ny, nz = lat[0:1], lat[1:2], lat[2:3]
    bx, by, bz = (jnp.where(n < 0, 1, 0) for n in (nx, ny, nz))
    cls = jnp.where(bx != by, 2, 0) + jnp.where(bx != bz, 1, 0)
    code = ((jnp.abs(nx) * 16 + jnp.abs(ny)) * 64 + cls * 16 + jnp.abs(nz)).astype(F32)
    masked = jnp.transpose(feat_ref[...].astype(F32)) * mask_ref[...].astype(F32)
    for b in range(2):
        head[own + b] = jnp.zeros((8, 128), F32)
        head[own + b, 0:3] = pos_ref[:, b * 128 : (b + 1) * 128]
        for r in range(3):
            at = (b * 3 + r) * 128
            head[own + b, 3 + r : 4 + r] = code[:, at : at + 128]
        feats[own + b] = masked[:, b * 128 : (b + 1) * 128].astype(BF16)
    acc[...] = jnp.zeros_like(acc)
    pres[...] = jnp.zeros_like(pres)
    kft[...] = jnp.transpose(kfilter_ref[...])
    pl.semaphore_wait(barrier, 16)

    def shard(ref, at):
        return ref.at[pl.ds(at, 2)]

    def send(src, dst, ss, rs, dev):
        return pltpu.make_async_remote_copy(
            src_ref=src, dst_ref=dst, send_sem=ss, recv_sem=rs, device_id=dev, device_id_type=MESH
        )

    def group_head(d, kk):
        r = shard(head, at_core(core, kk))
        return send(r, r, g_hs.at[d], g_hr.at[kk], (a, kpeer(d)))

    def group_feat(d, kk):
        r = shard(feats, at_core(core, kk))
        return send(r, r, g_fs.at[d], g_fr.at[kk], (a, kpeer(d)))

    def sib_head(c, kk):
        r = shard(head, at_core(c, kk))
        return send(r, r, s_hs.at[kk], s_hr.at[kk], sib)

    def sib_feat(c, kk):
        r = shard(feats, at_core(c, kk))
        return send(r, r, s_fs.at[kk], s_fr.at[kk], sib)

    def halo(ref, i):
        return send(shard(ref, own), shard(ref, at_halo(other, k)), h_s.at[i], h_r.at[i], halo_dev)

    def halo_in(ref, i):
        r = shard(ref, at_halo(core, k))
        return send(r, r, h_s.at[i], h_r.at[i], halo_dev)

    def spread(ref, d, kk, ss, rs):
        r = shard(ref, at_halo(core, kk))
        return send(r, r, ss.at[d], rs.at[kk], (a, kpeer(d)))

    sib_head(core, k).start()
    sib_feat(core, k).start()
    for d in range(1, 8):
        group_head(d, k).start()
    for d in range(1, 8):
        group_feat(d, k).start()
    halo(head, 0).start()
    halo(feats, 1).start()

    def row_numbers(rows):
        return lax.broadcasted_iota(jnp.int32, (rows, 512), 0)

    numbers = jnp.concatenate(
        [row_numbers(16), row_numbers(8) + 8 * core, 2 * k + lax.rem(row_numbers(8), 2)], axis=0
    ).astype(F32) * 0.125
    xy_rows = lax.broadcasted_iota(jnp.int32, (128, 1536), 0) + 128 * core
    zr = lax.broadcasted_iota(jnp.int32, (16, 1536), 0)
    z_rows = (zr // 2) * 16 + 2 * k + lax.rem(zr, 2)

    def gather_step(kk):
        blocks = [head[at_core(c, kk) + b] for c in range(2) for b in range(2)]
        px, py, pz = (jnp.concatenate([h[i : i + 1] for h in blocks], axis=1) for i in range(3))
        coord = jnp.concatenate(
            [jnp.broadcast_to(py, (16, 512)), jnp.broadcast_to(px, (8, 512)), jnp.broadcast_to(pz, (8, 512))],
            axis=0,
        )
        sines, cosines = sincos_turns(coord * numbers)
        fy = (cosines[0:16], sines[0:16])
        for tx, fx in enumerate((cosines[16:24], sines[16:24])):
            for ix in range(8):
                row = fx[ix : ix + 1]
                for ty in range(2):
                    at = ((tx * 2 + ty) * 8 + ix) * 16
                    tabs[kk, at : at + 16] = (row * fy[ty]).astype(BF16)
        fz = (cosines[24:25], cosines[25:26], sines[24:25], sines[25:26])
        rows = jnp.concatenate([feats[at_core(c, kk) + b] for c in range(2) for b in range(2)], axis=1)
        rows = rows.astype(F32)
        for i in range(4):
            ztab[kk, i : i + 1] = fz[i]
            zm[i * 128 : (i + 1) * 128] = (rows * fz[i]).astype(BF16)
        acc[...] += lax.dot_general(zm[...], tabs[kk], NT, preferred_element_type=F32)
        codes = jnp.concatenate([h[3 + r : 4 + r] for h in blocks for r in range(3)], axis=1).astype(jnp.int32)
        hot_xy = jnp.where((codes // 64) == xy_rows, 1.0, 0.0).astype(BF16)
        hot_z = jnp.where(lax.rem(codes, 64) == z_rows, 1.0, 0.0).astype(BF16)
        pres[...] += lax.dot_general(hot_z, hot_xy, NT, preferred_element_type=F32)

    sib_head(other, k).wait_recv()
    sib_feat(other, k).wait_recv()
    gather_step(k)

    def gather_loop(d, carry):
        kk = kpeer(d)
        group_head(d, kk).wait_recv()
        sib_head(core, kk).start()
        group_feat(d, kk).wait_recv()
        sib_feat(core, kk).start()
        sib_head(other, kk).wait_recv()
        sib_feat(other, kk).wait_recv()
        gather_step(kk)
        return carry

    lax.fori_loop(1, 8, gather_loop, 0)

    def rs_copy(d, src, slot):
        return send(pbuf.at[src], rbuf.at[slot], r_s.at[d], r_r.at[slot], (gpeer(d) * 2 + core, k))

    for d in range(1, 8):
        t = gpeer(d)
        for i in range(4):
            rows = pl.ds(pl.multiple_of(i * 128 + 16 * t, 16), 16)
            pbuf[t, i * 16 : (i + 1) * 16] = acc[rows].astype(BF16)
        rs_copy(d, t, g).start()

    halo_in(head, 0).wait_recv()
    for d in range(1, 8):
        spread(head, d, k, x_hs, x_hr).start()
    halo_in(feats, 1).wait_recv()
    for d in range(1, 8):
        spread(feats, d, k, x_fs, x_fr).start()

    eye = jnp.where(
        lax.broadcasted_iota(jnp.int32, (128, 128), 0) == lax.broadcasted_iota(jnp.int32, (128, 128), 1), 1.0, 0.0
    )

    def pair_step(b):
        me = jnp.transpose(head[own + b])
        mx, my, mz = me[:, 0:1], me[:, 1:2], me[:, 2:3]
        my_block = a * 16 + 2 * k + b

        def one(n, carry):
            ident = nb_ref[b, n]
            at = jnp.clip((ident - (2 * g - 1) * 16 + 256) % 256, 0, 63)
            h = head[at]
            same = jnp.where(ident == my_block, 1.0, 0.0)
            dx, dy, dz = mx - h[0:1], my - h[1:2], mz - h[2:3]
            d2 = dx * dx + dy * dy + dz * dz
            u = jnp.sqrt(d2) * (8.0 / 12.0)
            env = (1.0 - eye * same) * float(NS * BLK) ** -0.5 / (1.0 + d2 * (1.0 / 16.0))
            v = u - 0.5
            level = jnp.exp(v * v * -0.5) * env
            ratio = jnp.exp(u - 4.0)
            cols = pl.ds(pl.multiple_of(n * 128, 128), 128)
            for i in range(KB):
                basis[i * 128 : (i + 1) * 128, cols] = level.astype(BF16)
                if i < KB - 1:
                    level = level * ratio
            near[:, cols] = feats[at]
            return carry

        lax.fori_loop(0, NS, one, 0)
        sums = lax.dot_general(basis[...], near[...], NT, preferred_element_type=F32)
        for i in range(KB):
            scale = math.exp(4.0 * i - 0.5 * i * (i + 1))
            summed[:, i * 128 : (i + 1) * 128] = (sums[i * 128 : (i + 1) * 128] * scale).astype(BF16)
        pair[b * 128 : (b + 1) * 128] = jnp.dot(summed[...], pw_ref[...], preferred_element_type=F32)

    for d in range(1, 8):
        spread(head, d, kpeer(d), x_hs, x_hr).wait_recv()
        spread(feats, d, kpeer(d), x_fs, x_fr).wait_recv()
    pair_step(0)

    for d in range(1, 8):
        rs_copy(d, gpeer(d), gpeer(d)).wait_recv()
    factor = []
    for i in range(4):
        total = acc[pl.ds(pl.multiple_of(i * 128 + 16 * g, 16), 16)]
        for d in range(1, 8):
            total += rbuf[gpeer(d), i * 16 : (i + 1) * 16].astype(F32)
        factor.append(total)

    lane = lax.broadcasted_iota(jnp.int32, (8, 128), 1)
    abs_x = (lane // 16 + 8 * core).astype(F32)
    abs_y = lax.rem(lane, 16).astype(F32)
    kappa = (lax.broadcasted_iota(jnp.int32, (8, 128), 0).astype(F32) + 0.5) * (21.0 / KQ)
    coefs = kft[pl.ds(pl.multiple_of(16 * g, 16), 16)]
    for j in range(2):
        abs_z = (2 * k + j).astype(F32)
        mag = jnp.sqrt(abs_x * abs_x + abs_y * abs_y + abs_z * abs_z) * (2.0 * math.pi / 8.0)
        radial = (mag - kappa) * (KQ / 21.0)
        radial = jnp.exp(radial * radial * -0.5)
        kfilt = jnp.zeros((16, 128), F32)
        for p in range(KQ):
            kfilt += coefs[:, p : p + 1] * radial[p : p + 1]
        kfilt = kfilt * float(ATOMS * KW) ** -0.5

        def f(tz, tx, ty):
            at = (tx * 2 + ty) * 128
            return factor[tz * 2 + j][:, at : at + 128]

        even = (f(0, 0, 0), f(1, 0, 1), f(1, 1, 0), f(0, 1, 1))
        odd = (f(0, 1, 0), f(0, 0, 1), f(1, 0, 0), f(1, 1, 1))
        out_even = [0.0] * 4
        out_odd = [0.0] * 4
        for cl in range(4):
            pxy, pxz = 1.0 - 2.0 * (cl // 2), 1.0 - 2.0 * (cl % 2)
            pyz = pxy * pxz
            weight = pres[cl * 2 + j : cl * 2 + j + 1] * kfilt
            for parts, out, signs in (
                (even, out_even, (1.0, -pyz, -pxz, -pxy)),
                (odd, out_odd, (1.0, pxy, pxz, -pyz)),
            ):
                value = parts[0]
                for s, p in zip(signs[1:], parts[1:]):
                    value = value + p if s > 0 else value - p
                value = value * weight
                for i in range(4):
                    out[i] = out[i] + value if signs[i] > 0 else out[i] - value
        for (tz, tx, ty), value in zip(
            ((0, 0, 0), (1, 0, 1), (1, 1, 0), (0, 1, 1), (0, 1, 0), (0, 0, 1), (1, 0, 0), (1, 1, 1)),
            out_even + out_odd,
        ):
            at = (tx * 2 + ty) * 128
            rows = (tz * 2 + j) * 16
            gbuf[g, rows : rows + 16, at : at + 128] = value.astype(BF16)

    def ag_copy(d, slot):
        return send(gbuf.at[slot], gbuf.at[slot], a_s.at[d], a_r.at[slot], (gpeer(d) * 2 + core, k))

    for d in range(1, 8):
        ag_copy(d, g).start()
    pair_step(1)
    for d in range(1, 8):
        ag_copy(d, gpeer(d)).wait_recv()

    def sib_part(kk):
        return send(sibs.at[kk], sibin.at[kk], b_s.at[kk], b_r.at[kk], sib)

    def own_part(d, src, slot):
        return send(lsend.at[src], lbuf.at[slot], l_s.at[d], l_r.at[slot], (a, kpeer(d)))

    def message(kk):
        values = jnp.dot(gbuf[...].reshape(512, 512), tabs[kk], preferred_element_type=F32)
        fz = [ztab[kk, i : i + 1] for i in range(4)]
        for t in range(8):
            total = values[t * 64 : t * 64 + 16] * fz[0]
            for i in range(1, 4):
                total += values[t * 64 + i * 16 : t * 64 + (i + 1) * 16] * fz[i]
            part[0, t * 16 : (t + 1) * 16] = total[:, 0:256]
            part[1, t * 16 : (t + 1) * 16] = total[:, 256:512]
        lown[kk] = part[core]
        sibs[kk] = part[other].astype(BF16)
        sib_part(kk).start()

    def passed_on(d):
        kk = kpeer(d)
        sib_part(kk).wait_recv()
        lsend[kk] = (lown[kk] + sibin[kk].astype(F32)).astype(BF16)
        own_part(d, kk, k).start()

    message(kpeer(1))

    def message_loop(d, carry):
        message(kpeer(d))
        passed_on(d - 1)
        return carry

    lax.fori_loop(2, 8, message_loop, 0)
    message(k)
    passed_on(7)
    sib_part(k).wait_recv()
    long = lown[k] + sibin[k].astype(F32)
    for d in range(1, 8):
        own_part(d, kpeer(d), kpeer(d)).wait_recv()
        long += lbuf[kpeer(d)].astype(F32)

    total = feat_ref[...].astype(F32) + pair[...] + jnp.transpose(long)
    mean = jnp.mean(total * total, axis=-1, keepdims=True)
    normed = (total * lax.rsqrt(mean + 1e-6) * gain_ref[...]).astype(BF16)
    hidden = jnp.dot(normed, win_ref[...], preferred_element_type=F32)
    hidden = (hidden / (1.0 + jnp.exp(-hidden))).astype(BF16)
    out_ref[...] = (total + jnp.dot(hidden, wout_ref[...], preferred_element_type=F32)).astype(BF16)

    sib_head(core, k).wait_send()
    sib_feat(core, k).wait_send()
    halo(head, 0).wait_send()
    halo(feats, 1).wait_send()
    sib_part(k).wait_send()
    for d in range(1, 8):
        kk = kpeer(d)
        group_head(d, k).wait_send()
        group_feat(d, k).wait_send()
        sib_head(core, kk).wait_send()
        sib_feat(core, kk).wait_send()
        spread(head, d, k, x_hs, x_hr).wait_send()
        spread(feats, d, k, x_fs, x_fr).wait_send()
        rs_copy(d, gpeer(d), g).wait_send()
        ag_copy(d, g).wait_send()
        sib_part(kk).wait_send()
        own_part(d, kk, k).wait_send()


def per_device(positions, features, atom_mask, neighbours, lattice, pair_weight, kfilter, norm_gain, w_in, w_out):
    vmem = pl.BlockSpec(memory_space=pltpu.VMEM)
    smem = pl.BlockSpec(memory_space=pltpu.SMEM)
    dma = pltpu.SemaphoreType.DMA((8,))
    return pl.pallas_call(
        kernel,
        out_shape=jax.ShapeDtypeStruct(features.shape, BF16),
        in_specs=[vmem, vmem, vmem, smem] + [vmem] * 6,
        out_specs=vmem,
        scratch_shapes=[
            pltpu.VMEM((64, 8, 128), F32),
            pltpu.VMEM((64, 128, 128), BF16),
            pltpu.VMEM((8, 512, 512), BF16),
            pltpu.VMEM((8, 8, 512), F32),
            pltpu.VMEM((512, 512), BF16),
            pltpu.VMEM((512, 512), F32),
            pltpu.VMEM((16, 128), F32),
            pltpu.VMEM((128, 8), F32),
            pltpu.VMEM((8, 64, 512), BF16),
            pltpu.VMEM((8, 64, 512), BF16),
            pltpu.VMEM((8, 64, 512), BF16),
            pltpu.VMEM((2, 128, 256), F32),
            pltpu.VMEM((8, 128, 256), F32),
            pltpu.VMEM((8, 128, 256), BF16),
            pltpu.VMEM((8, 128, 256), BF16),
            pltpu.VMEM((8, 128, 256), BF16),
            pltpu.VMEM((8, 128, 256), BF16),
            pltpu.VMEM((1024, 1536), BF16),
            pltpu.VMEM((128, 1536), BF16),
            pltpu.VMEM((128, 1024), BF16),
            pltpu.VMEM((256, 128), F32),
        ]
        + [dma] * 8
        + [pltpu.SemaphoreType.DMA((2,))] * 2
        + [dma] * 12,
        compiler_params=pltpu.CompilerParams(
            collective_id=0, has_side_effects=True, vmem_limit_bytes=48 * 1024 * 1024
        ),
    )(
        positions, features, atom_mask.reshape(1, -1), neighbours, lattice, pair_weight, kfilter,
        norm_gain.reshape(1, -1), w_in, w_out,
    )


def solution(mesh):
    return jax.shard_map(
        per_device,
        mesh=mesh,
        in_specs=(
            P(None, ("atoms", "kvec")),
            P(("atoms", "kvec"), None),
            P(("atoms", "kvec")),
            P(("atoms", "kvec"), None),
            P(None, "kvec"),
            P(),
            P(),
            P(),
            P(),
            P(),
        ),
        out_specs=P(("atoms", "kvec"), None),
        check_vma=False,
    )
```

```python
import math

import jax
import jax.numpy as jnp
from jax import lax
from jax.experimental import pallas as pl
from jax.experimental.pallas import tpu as pltpu
from jax.sharding import PartitionSpec as P

MESH = pl.DeviceIdType.MESH
F32 = jnp.float32
BF16 = jnp.bfloat16
KW = 12288
BLK = 128
C = 128
KB = 8
KQ = 8
NS = 12
ATOMS = 32768
NT = (((1,), (1,)), ((), ()))

SIN = tuple((-1.0) ** i / math.factorial(2 * i + 1) for i in range(6))
COS = tuple((-1.0) ** i / math.factorial(2 * i) for i in range(7))


def poly(h2, coefs):
    total = h2 * coefs[-1] + coefs[-2]
    for c in coefs[-3::-1]:
        total = total * h2 + c
    return total


def sincos_turns(turns):
    h = (turns - jnp.floor(turns + 0.5)) * math.pi
    h2 = h * h
    s = h * poly(h2, SIN)
    c = poly(h2, COS)
    return 2.0 * s * c, 1.0 - 2.0 * s * s


def kernel(
    pos_in, feat_in, mask_in, nb_in, lat_in, pw_in, kfilter_in, gain_in, win_in, wout_in,
    out_ref,
    pos_ref, feat_ref, mask_ref, nb_ref, lat_ref, pw_ref, kfilter_ref, gain_ref, win_ref, wout_ref, in_sem,
    window, stage, tabs, ztab, zm, acc, pres, kft, pbuf, rbuf, gbuf, lown, sibs, sibin, lsend, lbuf,
    basis, near, summed, pair,
    g_s, g_r, s_s, s_r, h_s, h_r, x_s, x_r, r_s, r_r, a_s, a_r, b_s, b_r, l_s, l_r,
):
    a = lax.axis_index("atoms")
    k = lax.axis_index("kvec")
    core = lax.rem(a, 2)
    g = a // 2
    other = 1 - core
    sib = (g * 2 + other, k)

    def kpeer(d):
        return ((k // 4 + d // 4) % 2) * 4 + (k % 4 + d % 4) % 4

    def gpeer(d):
        return ((g // 4 + d // 4) % 2) * 4 + (g % 4 + d % 4) % 4

    halo_dev = (((g + jnp.where(core == 1, 1, 7)) % 8) * 2 + other, k)

    loads = [
        pltpu.make_async_copy(src, dst, in_sem.at[i])
        for i, (src, dst) in enumerate((
            (lat_in, lat_ref), (feat_in, feat_ref), (mask_in, mask_ref), (pos_in, pos_ref), (kfilter_in, kfilter_ref),
            (nb_in, nb_ref), (pw_in, pw_ref), (gain_in, gain_ref), (win_in, win_ref), (wout_in, wout_ref),
        ))
    ]
    barrier = pltpu.get_barrier_semaphore()
    for d in range(1, 8):
        pl.semaphore_signal(barrier, inc=1, device_id=(gpeer(d) * 2 + core, k), device_id_type=MESH)
        pl.semaphore_signal(barrier, inc=1, device_id=(a, kpeer(d)), device_id_type=MESH)
    pl.semaphore_signal(barrier, inc=1, device_id=halo_dev, device_id_type=MESH)
    pl.semaphore_signal(barrier, inc=1, device_id=sib, device_id_type=MESH)
    for load in loads:
        load.start()

    def at_core(c, kk):
        return 16 + c * 16 + 2 * kk

    def at_halo(c, kk):
        return c * 48 + 2 * kk

    own = at_core(core, k)
    acc[...] = jnp.zeros_like(acc)
    pres[...] = jnp.zeros_like(pres)
    for load in loads[:5]:
        load.wait()
    lat = lat_ref[:, pl.ds(pl.multiple_of(core * 768, 128), 768)]
    nx, ny, nz = lat[0:1], lat[1:2], lat[2:3]
    bx, by, bz = (jnp.where(n < 0, 1, 0) for n in (nx, ny, nz))
    cls = jnp.where(bx != by, 2, 0) + jnp.where(bx != bz, 1, 0)
    code_xy = (jnp.abs(nx) * 16 + jnp.abs(ny)).astype(F32)
    code_z = (cls * 16 + jnp.abs(nz)).astype(F32)
    masked = jnp.transpose(feat_ref[...].astype(F32)) * mask_ref[...].astype(F32)
    stage[...] = jnp.zeros_like(stage)
    for b in range(2):
        rest = pos_ref[:, b * 128 : (b + 1) * 128]
        for i in range(3):
            piece = rest.astype(BF16).astype(F32)
            stage[b, 3 * i : 3 * i + 3] = piece
            rest = rest - piece
        for r in range(3):
            at = (b * 3 + r) * 128
            stage[b, 9 + r : 10 + r] = code_xy[:, at : at + 128]
            stage[b, 12 + r : 13 + r] = code_z[:, at : at + 128]
        window[own + b, 0:16] = stage[b].astype(BF16)
        window[own + b, 16:144] = masked[:, b * 128 : (b + 1) * 128].astype(BF16)
    kft[...] = jnp.transpose(kfilter_ref[...])
    pl.semaphore_wait(barrier, 16)

    def half(at, h):
        return window.at[pl.ds(at, 2), pl.ds(80 * h, 80 - 16 * h)]

    def send(src, dst, ss, rs, dev):
        return pltpu.make_async_remote_copy(
            src_ref=src, dst_ref=dst, send_sem=ss, recv_sem=rs, device_id=dev, device_id_type=MESH
        )

    def group_copy(h, d, kk):
        r = half(at_core(core, kk), h)
        return send(r, r, g_s.at[h, d], g_r.at[h, kk], (a, kpeer(d)))

    def sib_copy(h, c, kk):
        r = half(at_core(c, kk), h)
        return send(r, r, s_s.at[h, kk], s_r.at[h, kk], sib)

    def halo_copy(src, dst):
        return send(window.at[pl.ds(src, 2)], window.at[pl.ds(dst, 2)], h_s.at[0], h_r.at[0], halo_dev)

    def spread(d, kk):
        r = window.at[pl.ds(at_halo(core, kk), 2)]
        return send(r, r, x_s.at[d], x_r.at[kk], (a, kpeer(d)))

    for h in range(2):
        for d in (6, 2, 5, 7, 1, 3, 4):
            group_copy(h, d, k).start()
        sib_copy(h, core, k).start()
    halo_copy(own, at_halo(other, k)).start()

    def row_numbers(rows):
        return lax.broadcasted_iota(jnp.int32, (rows, 512), 0)

    numbers = jnp.concatenate(
        [row_numbers(16), row_numbers(8) + 8 * core, 2 * k + lax.rem(row_numbers(8), 2)], axis=0
    ).astype(F32) * 0.125

    def joined(kk, low, count):
        return jnp.concatenate(
            [window[at_core(c, kk) + b, low : low + count] for c in range(2) for b in range(2)], axis=1
        ).astype(F32)

    def tables(kk):
        rows = joined(kk, 0, 16)
        px, py, pz = (rows[i : i + 1] + rows[i + 3 : i + 4] + rows[i + 6 : i + 7] for i in range(3))
        coord = jnp.concatenate(
            [jnp.broadcast_to(py, (16, 512)), jnp.broadcast_to(px, (8, 512)), jnp.broadcast_to(pz, (8, 512))],
            axis=0,
        )
        sines, cosines = sincos_turns(coord * numbers)
        fy = (cosines[0:16], sines[0:16])
        for tx, fx in enumerate((cosines[16:24], sines[16:24])):
            for ix in range(8):
                row = fx[ix : ix + 1]
                for ty in range(2):
                    at = ((tx * 2 + ty) * 8 + ix) * 16
                    tabs[kk, at : at + 16] = (row * fy[ty]).astype(BF16)
        for i, row in enumerate((cosines[24:25], cosines[25:26], sines[24:25], sines[25:26])):
            ztab[kk, i : i + 1] = row

    def factor_step(h, kk):
        rows = joined(kk, 16 + 64 * h, 64)
        for i in range(4):
            zm[i * 64 : (i + 1) * 64] = (rows * ztab[kk, i : i + 1]).astype(BF16)
        acc[h] += lax.dot_general(zm[...], tabs[kk], NT, preferred_element_type=F32)

    def arrive(h, kk):
        group_copy(h, 0, kk).wait_recv()
        sib_copy(h, core, kk).start()

    def use(h, kk):
        sib_copy(h, other, kk).wait_recv()
        if h == 0:
            tables(kk)
        factor_step(h, kk)

    def rs_copy(h, d, src, slot):
        return send(pbuf.at[h, src], rbuf.at[h, slot], r_s.at[h, d], r_r.at[h, slot], (gpeer(d) * 2 + core, k))

    def gather_half(h):
        def step(d, carry):
            arrive(h, kpeer(d))
            use(h, kpeer(d - 1))
            return carry

        lax.fori_loop(1, 8, step, 0)
        use(h, kpeer(7))
        for d in (6, 2, 5, 7, 1, 3, 4):
            t = gpeer(d)
            for i in range(0, 4, 2):
                rows = jnp.concatenate(
                    [acc[h, pl.ds(pl.multiple_of(j * 64 + 8 * t, 8), 8)] for j in (i, i + 1)], axis=0
                )
                pbuf[h, t, i * 8 : i * 8 + 16] = rows.astype(BF16)
            rs_copy(h, d, t, g).start()

    gather_half(0)
    gather_half(1)

    halo_copy(own, at_halo(core, k)).wait_recv()
    for d in (6, 2, 5, 7, 1, 3, 4):
        spread(d, k).start()

    xy_rows = lax.broadcasted_iota(jnp.int32, (128, 512), 0) + 128 * core
    zr = lax.broadcasted_iota(jnp.int32, (16, 512), 0)
    z_rows = ((zr // 2) * 16 + 2 * k + lax.rem(zr, 2)).astype(F32)
    xy_rows = xy_rows.astype(F32)

    def presence_step(kk, carry):
        rows = joined(kk, 0, 16)
        for r in range(3):
            hot_xy = jnp.where(rows[9 + r : 10 + r] == xy_rows, 1.0, 0.0).astype(BF16)
            hot_z = jnp.where(rows[12 + r : 13 + r] == z_rows, 1.0, 0.0).astype(BF16)
            pres[...] += lax.dot_general(hot_z, hot_xy, NT, preferred_element_type=F32)
        return carry

    lax.fori_loop(0, 8, presence_step, 0)

    lane = lax.broadcasted_iota(jnp.int32, (8, 128), 1)
    abs_x = (lane // 16 + 8 * core).astype(F32)
    abs_y = lax.rem(lane, 16).astype(F32)
    kappa = (lax.broadcasted_iota(jnp.int32, (8, 128), 0).astype(F32) + 0.5) * (21.0 / KQ)

    def filter_half(h):
        for d in range(1, 8):
            rs_copy(h, d, gpeer(d), gpeer(d)).wait_recv()
        factor = []
        for i in range(0, 4, 2):
            total = jnp.concatenate(
                [acc[h, pl.ds(pl.multiple_of(j * 64 + 8 * g, 8), 8)] for j in (i, i + 1)], axis=0
            )
            for d in range(1, 8):
                total += rbuf[h, gpeer(d), i * 8 : i * 8 + 16].astype(F32)
            factor += [total[0:8], total[8:16]]
        coefs = kft[pl.ds(pl.multiple_of(64 * h + 8 * g, 8), 8)]
        results = {}
        for j in range(2):
            abs_z = (2 * k + j).astype(F32)
            mag = jnp.sqrt(abs_x * abs_x + abs_y * abs_y + abs_z * abs_z) * (2.0 * math.pi / 8.0)
            radial = (mag - kappa) * (KQ / 21.0)
            radial = jnp.exp(radial * radial * -0.5)
            kfilt = jnp.zeros((8, 128), F32)
            for p in range(KQ):
                kfilt += coefs[:, p : p + 1] * radial[p : p + 1]
            kfilt = kfilt * float(ATOMS * KW) ** -0.5
            names = ((0, 0, 0), (1, 0, 1), (1, 1, 0), (0, 1, 1), (0, 1, 0), (0, 0, 1), (1, 0, 0), (1, 1, 1))
            values = [
                factor[tz * 2 + j][:, (tx * 2 + ty) * 128 : (tx * 2 + ty + 1) * 128] for tz, tx, ty in names
            ]
            even, odd = values[:4], values[4:]
            out_even = [0.0] * 4
            out_odd = [0.0] * 4
            for cl in range(4):
                pxy, pxz = 1.0 - 2.0 * (cl // 2), 1.0 - 2.0 * (cl % 2)
                pyz = pxy * pxz
                weight = pres[cl * 2 + j : cl * 2 + j + 1] * kfilt
                for parts, out, signs in (
                    (even, out_even, (1.0, -pyz, -pxz, -pxy)),
                    (odd, out_odd, (1.0, pxy, pxz, -pyz)),
                ):
                    value = parts[0]
                    for s, p in zip(signs[1:], parts[1:]):
                        value = value + p if s > 0 else value - p
                    value = value * weight
                    for i in range(4):
                        out[i] = out[i] + value if signs[i] > 0 else out[i] - value
            for (tz, tx, ty), value in zip(names, out_even + out_odd):
                results[tz, j, tx, ty] = value
        for tz in range(2):
            for tx in range(2):
                for ty in range(2):
                    at = (tx * 2 + ty) * 128
                    both = jnp.concatenate([results[tz, 0, tx, ty], results[tz, 1, tx, ty]], axis=0)
                    gbuf[h, g, tz * 16 : tz * 16 + 16, at : at + 128] = both.astype(BF16)
        for d in (6, 2, 5, 7, 1, 3, 4):
            ag_copy(h, d, g).start()

    def ag_copy(h, d, slot):
        r = gbuf.at[h, slot]
        return send(r, r, a_s.at[h, d], a_r.at[h, slot], (gpeer(d) * 2 + core, k))

    eye = jnp.where(
        lax.broadcasted_iota(jnp.int32, (128, 128), 0) == lax.broadcasted_iota(jnp.int32, (128, 128), 1), 1.0, 0.0
    )

    def pair_step(b):
        me = jnp.transpose(window[own + b, 0:16].astype(F32))
        mx, my, mz = (me[:, i : i + 1] + me[:, i + 3 : i + 4] + me[:, i + 6 : i + 7] for i in range(3))
        my_block = a * 16 + 2 * k + b

        def one(n, carry):
            ident = nb_ref[b, n]
            at = jnp.clip((ident - (2 * g - 1) * 16 + 256) % 256, 0, 63)
            r = window[at, 0:16].astype(F32)
            px, py, pz = (r[i : i + 1] + r[i + 3 : i + 4] + r[i + 6 : i + 7] for i in range(3))
            same = jnp.where(ident == my_block, 1.0, 0.0)
            dx, dy, dz = mx - px, my - py, mz - pz
            d2 = dx * dx + dy * dy + dz * dz
            u = jnp.sqrt(d2) * (8.0 / 12.0)
            env = (1.0 - eye * same) * float(NS * BLK) ** -0.5 / (1.0 + d2 * (1.0 / 16.0))
            v = u - 0.5
            level = jnp.exp(v * v * -0.5) * env
            ratio = jnp.exp(u - 4.0)
            cols = pl.ds(pl.multiple_of(n * 128, 128), 128)
            for i in range(KB):
                basis[i * 128 : (i + 1) * 128, cols] = level.astype(BF16)
                if i < KB - 1:
                    level = level * ratio
            near[:, cols] = window[at, 16:144]
            return carry

        lax.fori_loop(0, NS, one, 0)
        sums = lax.dot_general(basis[...], near[...], NT, preferred_element_type=F32)
        for i in range(KB):
            scale = math.exp(4.0 * i - 0.5 * i * (i + 1))
            summed[:, i * 128 : (i + 1) * 128] = (sums[i * 128 : (i + 1) * 128] * scale).astype(BF16)
        pair[b * 128 : (b + 1) * 128] = jnp.dot(summed[...], pw_ref[...], preferred_element_type=F32)

    filter_half(0)
    filter_half(1)
    for load in loads[5:7]:
        load.wait()
    for d in range(1, 8):
        spread(d, kpeer(d)).wait_recv()
    pair_step(0)

    def sib_part(h, kk):
        return send(sibs.at[h, kk], sibin.at[h, kk], b_s.at[h, kk], b_r.at[h, kk], sib)

    def own_part(h, d, src, slot):
        return send(lsend.at[h, src], lbuf.at[h, slot], l_s.at[h, d], l_r.at[h, slot], (a, kpeer(d)))

    def message(h, kk):
        values = jnp.dot(gbuf[h].reshape(256, 512), tabs[kk], preferred_element_type=F32)
        fz = [ztab[kk, i : i + 1] for i in range(4)]
        for t in range(0, 8, 2):
            pieces = []
            for u in (t, t + 1):
                total = values[u * 32 : u * 32 + 8] * fz[0]
                for i in range(1, 4):
                    total += values[u * 32 + i * 8 : u * 32 + (i + 1) * 8] * fz[i]
                pieces.append(total)
            both = jnp.concatenate(pieces, axis=0)
            low, high = both[:, 0:256], both[:, 256:512]
            lown[h, kk, t * 8 : t * 8 + 16] = jnp.where(core == 0, low, high)
            sibs[h, kk, t * 8 : t * 8 + 16] = jnp.where(core == 0, high, low).astype(BF16)
        sib_part(h, kk).start()

    def passed_on(h, d):
        kk = kpeer(d)
        sib_part(h, kk).wait_recv()
        lsend[h, kk] = (lown[h, kk] + sibin[h, kk].astype(F32)).astype(BF16)
        own_part(h, d, kk, k).start()

    for h in range(2):
        for d in range(1, 8):
            ag_copy(h, d, gpeer(d)).wait_recv()
        message(h, kpeer(7))
        message(h, kpeer(6))

        def message_loop(i, carry):
            message(h, kpeer(7 - i))
            passed_on(h, 9 - i)
            return carry

        lax.fori_loop(2, 7, message_loop, 0)
        message(h, k)
        passed_on(h, 2)
        passed_on(h, 1)

    pair_step(1)
    rest = feat_ref[...].astype(F32) + pair[...]
    for load in loads[7:]:
        load.wait()
    longs = []
    for h in range(2):
        sib_part(h, k).wait_recv()
        long = lown[h, k] + sibin[h, k].astype(F32)
        for d in range(1, 8):
            own_part(h, d, kpeer(d), kpeer(d)).wait_recv()
            long += lbuf[h, kpeer(d)].astype(F32)
        longs.append(long)

    total = rest + jnp.transpose(jnp.concatenate(longs, axis=0))
    mean = jnp.mean(total * total, axis=-1, keepdims=True)
    normed = (total * lax.rsqrt(mean + 1e-6) * gain_ref[...]).astype(BF16)
    hidden = jnp.dot(normed, win_ref[...], preferred_element_type=F32)
    hidden = (hidden / (1.0 + jnp.exp(-hidden))).astype(BF16)
    out_ref[...] = (total + jnp.dot(hidden, wout_ref[...], preferred_element_type=F32)).astype(BF16)

    halo_copy(own, at_halo(other, k)).wait_send()
    for h in range(2):
        sib_copy(h, core, k).wait_send()
        sib_part(h, k).wait_send()
        for d in range(1, 8):
            kk = kpeer(d)
            group_copy(h, d, k).wait_send()
            sib_copy(h, core, kk).wait_send()
            rs_copy(h, d, gpeer(d), g).wait_send()
            ag_copy(h, d, g).wait_send()
            sib_part(h, kk).wait_send()
            own_part(h, d, kk, k).wait_send()
    for d in range(1, 8):
        spread(d, k).wait_send()


def per_device(positions, features, atom_mask, neighbours, lattice, pair_weight, kfilter, norm_gain, w_in, w_out):
    dma = pltpu.SemaphoreType.DMA((2, 8))
    operands = (
        positions, features, atom_mask.reshape(1, -1), neighbours, lattice, pair_weight, kfilter,
        norm_gain.reshape(1, -1), w_in, w_out,
    )
    return pl.pallas_call(
        kernel,
        out_shape=jax.ShapeDtypeStruct(features.shape, BF16),
        in_specs=[pl.BlockSpec(memory_space=pl.ANY)] * len(operands),
        out_specs=pl.BlockSpec(memory_space=pltpu.VMEM),
        scratch_shapes=[
            (pltpu.SMEM if x is neighbours else pltpu.VMEM)(x.shape, x.dtype) for x in operands
        ]
        + [
            pltpu.SemaphoreType.DMA((10,)),
            pltpu.VMEM((64, 144, 128), BF16),
            pltpu.VMEM((2, 16, 128), F32),
            pltpu.VMEM((8, 512, 512), BF16),
            pltpu.VMEM((8, 8, 512), F32),
            pltpu.VMEM((256, 512), BF16),
            pltpu.VMEM((2, 256, 512), F32),
            pltpu.VMEM((16, 128), F32),
            pltpu.VMEM((128, 8), F32),
            pltpu.VMEM((2, 8, 32, 512), BF16),
            pltpu.VMEM((2, 8, 32, 512), BF16),
            pltpu.VMEM((2, 8, 32, 512), BF16),
            pltpu.VMEM((2, 8, 64, 256), F32),
            pltpu.VMEM((2, 8, 64, 256), BF16),
            pltpu.VMEM((2, 8, 64, 256), BF16),
            pltpu.VMEM((2, 8, 64, 256), BF16),
            pltpu.VMEM((2, 8, 64, 256), BF16),
            pltpu.VMEM((1024, 1536), BF16),
            pltpu.VMEM((128, 1536), BF16),
            pltpu.VMEM((128, 1024), BF16),
            pltpu.VMEM((256, 128), F32),
        ]
        + [dma] * 4
        + [pltpu.SemaphoreType.DMA((1,))] * 2
        + [pltpu.SemaphoreType.DMA((8,))] * 2
        + [dma] * 8,
        compiler_params=pltpu.CompilerParams(
            collective_id=0, has_side_effects=True, vmem_limit_bytes=56 * 1024 * 1024
        ),
    )(*operands)


def solution(mesh):
    return jax.shard_map(
        per_device,
        mesh=mesh,
        in_specs=(
            P(None, ("atoms", "kvec")),
            P(("atoms", "kvec"), None),
            P(("atoms", "kvec")),
            P(("atoms", "kvec"), None),
            P(None, "kvec"),
            P(),
            P(),
            P(),
            P(),
            P(),
        ),
        out_specs=P(("atoms", "kvec"), None),
        check_vma=False,
    )
```

```python
import math

import jax
import jax.numpy as jnp
from jax import lax
from jax.experimental import pallas as pl
from jax.experimental.pallas import tpu as pltpu
from jax.sharding import PartitionSpec as P

MESH = pl.DeviceIdType.MESH
F32 = jnp.float32
BF16 = jnp.bfloat16
KW = 12288
BLK = 128
C = 128
KB = 8
KQ = 8
NS = 12
ATOMS = 32768
NT = (((1,), (1,)), ((), ()))

SIN = tuple((-1.0) ** i / math.factorial(2 * i + 1) for i in range(6))
COS = tuple((-1.0) ** i / math.factorial(2 * i) for i in range(7))


def poly(h2, coefs):
    total = h2 * coefs[-1] + coefs[-2]
    for c in coefs[-3::-1]:
        total = total * h2 + c
    return total


def sincos_turns(turns):
    h = (turns - jnp.floor(turns + 0.5)) * math.pi
    h2 = h * h
    s = h * poly(h2, SIN)
    c = poly(h2, COS)
    return 2.0 * s * c, 1.0 - 2.0 * s * s


def kernel(
    pos_in, feat_in, mask_in, nb_in, lat_in, pw_in, kfilter_in, gain_in, win_in, wout_in,
    out_ref,
    pos_ref, feat_ref, mask_ref, nb_ref, lat_ref, pw_ref, kfilter_ref, gain_ref, win_ref, wout_ref, in_sem,
    window, stage, tabs, ztab, zm, acc, pres, kft, pbuf, rbuf, gbuf, lown, sibs, sibin, lsend, lbuf,
    basis, near, summed, pair,
    g_s, g_r, s_s, s_r, h_s, h_r, x_s, x_r, r_s, r_r, a_s, a_r, b_s, b_r, l_s, l_r,
):
    a = lax.axis_index("atoms")
    k = lax.axis_index("kvec")
    core = lax.rem(a, 2)
    g = a // 2
    other = 1 - core
    sib = (g * 2 + other, k)

    def kpeer(d):
        return ((k // 4 + d // 4) % 2) * 4 + (k % 4 + d % 4) % 4

    def gpeer(d):
        return ((g // 4 + d // 4) % 2) * 4 + (g % 4 + d % 4) % 4

    halo_dev = (((g + jnp.where(core == 1, 1, 7)) % 8) * 2 + other, k)

    loads = [
        pltpu.make_async_copy(src, dst, in_sem.at[i])
        for i, (src, dst) in enumerate((
            (lat_in, lat_ref), (feat_in, feat_ref), (mask_in, mask_ref), (pos_in, pos_ref), (kfilter_in, kfilter_ref),
            (nb_in, nb_ref), (pw_in, pw_ref), (gain_in, gain_ref), (win_in, win_ref), (wout_in, wout_ref),
        ))
    ]
    barrier = pltpu.get_barrier_semaphore()
    for d in range(1, 8):
        pl.semaphore_signal(barrier, inc=1, device_id=(gpeer(d) * 2 + core, k), device_id_type=MESH)
        pl.semaphore_signal(barrier, inc=1, device_id=(a, kpeer(d)), device_id_type=MESH)
    pl.semaphore_signal(barrier, inc=1, device_id=halo_dev, device_id_type=MESH)
    pl.semaphore_signal(barrier, inc=1, device_id=sib, device_id_type=MESH)
    for load in loads:
        load.start()

    def at_core(c, kk):
        return 16 + c * 16 + 2 * kk

    def at_halo(c, kk):
        return c * 48 + 2 * kk

    own = at_core(core, k)
    acc[...] = jnp.zeros_like(acc)
    pres[...] = jnp.zeros_like(pres)
    for load in loads[:5]:
        load.wait()
    lat = lat_ref[:, pl.ds(pl.multiple_of(core * 768, 128), 768)]
    nx, ny, nz = lat[0:1], lat[1:2], lat[2:3]
    bx, by, bz = (jnp.where(n < 0, 1, 0) for n in (nx, ny, nz))
    cls = jnp.where(bx != by, 2, 0) + jnp.where(bx != bz, 1, 0)
    code_xy = (jnp.abs(nx) * 16 + jnp.abs(ny)).astype(F32)
    code_z = (cls * 16 + jnp.abs(nz)).astype(F32)
    masked = jnp.transpose(feat_ref[...].astype(F32)) * mask_ref[...].astype(F32)
    stage[...] = jnp.zeros_like(stage)
    for b in range(2):
        rest = pos_ref[:, b * 128 : (b + 1) * 128]
        for i in range(3):
            piece = rest.astype(BF16).astype(F32)
            stage[b, 3 * i : 3 * i + 3] = piece
            rest = rest - piece
        for r in range(3):
            at = (b * 3 + r) * 128
            stage[b, 9 + r : 10 + r] = code_xy[:, at : at + 128]
            stage[b, 12 + r : 13 + r] = code_z[:, at : at + 128]
        window[own + b, 0:16] = stage[b].astype(BF16)
        window[own + b, 16:144] = masked[:, b * 128 : (b + 1) * 128].astype(BF16)
    kft[...] = jnp.transpose(kfilter_ref[...])
    pl.semaphore_wait(barrier, 16)

    def half(at, h):
        return window.at[pl.ds(at, 2), pl.ds(80 * h, 80 - 16 * h)]

    def send(src, dst, ss, rs, dev):
        return pltpu.make_async_remote_copy(
            src_ref=src, dst_ref=dst, send_sem=ss, recv_sem=rs, device_id=dev, device_id_type=MESH
        )

    def group_copy(h, d, kk):
        r = half(at_core(core, kk), h)
        return send(r, r, g_s.at[h, d], g_r.at[h, kk], (a, kpeer(d)))

    def sib_copy(h, c, kk):
        r = half(at_core(c, kk), h)
        return send(r, r, s_s.at[h, kk], s_r.at[h, kk], sib)

    def halo_copy(src, dst):
        return send(window.at[pl.ds(src, 2)], window.at[pl.ds(dst, 2)], h_s.at[0], h_r.at[0], halo_dev)

    ky = (k + 4) % 8

    def spread(d, kk):
        r = window.at[pl.ds(at_halo(core, kk), 2)]
        at = d - 1 if kk is k else d + 3
        return send(r, r, x_s.at[at], x_r.at[kk], (a, kpeer(d)))

    sib_copy(0, core, k).start()
    for d in range(1, 8):
        group_copy(0, d, k).start()
    halo_copy(own, at_halo(other, k)).start()
    sib_copy(1, core, k).start()

    def row_numbers(rows):
        return lax.broadcasted_iota(jnp.int32, (rows, 512), 0)

    numbers = jnp.concatenate(
        [row_numbers(16), row_numbers(8) + 8 * core, 2 * k + lax.rem(row_numbers(8), 2)], axis=0
    ).astype(F32) * 0.125

    def joined(kk, low, count):
        return jnp.concatenate(
            [window[at_core(c, kk) + b, low : low + count] for c in range(2) for b in range(2)], axis=1
        ).astype(F32)

    def tables(kk):
        rows = joined(kk, 0, 16)
        px, py, pz = (rows[i : i + 1] + rows[i + 3 : i + 4] + rows[i + 6 : i + 7] for i in range(3))
        coord = jnp.concatenate(
            [jnp.broadcast_to(py, (16, 512)), jnp.broadcast_to(px, (8, 512)), jnp.broadcast_to(pz, (8, 512))],
            axis=0,
        )
        sines, cosines = sincos_turns(coord * numbers)
        fy = (cosines[0:16], sines[0:16])
        for tx, fx in enumerate((cosines[16:24], sines[16:24])):
            for ix in range(8):
                row = fx[ix : ix + 1]
                for ty in range(2):
                    at = ((tx * 2 + ty) * 8 + ix) * 16
                    tabs[kk, at : at + 16] = (row * fy[ty]).astype(BF16)
        for i, row in enumerate((cosines[24:25], cosines[25:26], sines[24:25], sines[25:26])):
            ztab[kk, i : i + 1] = row

    def factor_step(h, kk):
        rows = joined(kk, 16 + 64 * h, 64)
        for i in range(4):
            zm[i * 64 : (i + 1) * 64] = (rows * ztab[kk, i : i + 1]).astype(BF16)
        acc[h] += lax.dot_general(zm[...], tabs[kk], NT, preferred_element_type=F32)

    def arrive(h, d):
        kk = kpeer(d)
        group_copy(h, 0, kk).wait_recv()
        sib_copy(h, core, kk).start()
        if h == 0:
            group_copy(1, d, k).start()

    def use(h, kk):
        sib_copy(h, other, kk).wait_recv()
        if h == 0:
            tables(kk)
        factor_step(h, kk)

    def rs_copy(h, d, src, slot):
        return send(pbuf.at[h, src], rbuf.at[h, slot], r_s.at[h, d], r_r.at[h, slot], (gpeer(d) * 2 + core, k))

    def gather_half(h):
        def step(d, carry):
            arrive(h, d)
            use(h, kpeer(d - 1))
            return carry

        lax.fori_loop(1, 8, step, 0)
        use(h, kpeer(7))
        for d in (6, 2, 5, 7, 1, 3, 4):
            t = gpeer(d)
            for i in range(0, 4, 2):
                rows = jnp.concatenate(
                    [acc[h, pl.ds(pl.multiple_of(j * 64 + 8 * t, 8), 8)] for j in (i, i + 1)], axis=0
                )
                pbuf[h, t, i * 8 : i * 8 + 16] = rows.astype(BF16)
            rs_copy(h, d, t, g).start()

    gather_half(0)
    gather_half(1)


    halo_copy(own, at_halo(core, k)).wait_recv()
    for d in (4, 1, 3, 2):
        spread(d, k).start()

    xy_rows = lax.broadcasted_iota(jnp.int32, (128, 512), 0) + 128 * core
    zr = lax.broadcasted_iota(jnp.int32, (16, 512), 0)
    z_rows = ((zr // 2) * 16 + 2 * k + lax.rem(zr, 2)).astype(F32)
    xy_rows = xy_rows.astype(F32)

    def presence_step(kk, carry):
        rows = joined(kk, 0, 16)
        for r in range(3):
            hot_xy = jnp.where(rows[9 + r : 10 + r] == xy_rows, 1.0, 0.0).astype(BF16)
            hot_z = jnp.where(rows[12 + r : 13 + r] == z_rows, 1.0, 0.0).astype(BF16)
            pres[...] += lax.dot_general(hot_z, hot_xy, NT, preferred_element_type=F32)
        return carry

    lax.fori_loop(0, 8, presence_step, 0)

    lane = lax.broadcasted_iota(jnp.int32, (8, 128), 1)
    abs_x = (lane // 16 + 8 * core).astype(F32)
    abs_y = lax.rem(lane, 16).astype(F32)
    kappa = (lax.broadcasted_iota(jnp.int32, (8, 128), 0).astype(F32) + 0.5) * (21.0 / KQ)

    def filter_half(h):
        for d in range(1, 8):
            rs_copy(h, d, gpeer(d), gpeer(d)).wait_recv()
        factor = []
        for i in range(0, 4, 2):
            total = jnp.concatenate(
                [acc[h, pl.ds(pl.multiple_of(j * 64 + 8 * g, 8), 8)] for j in (i, i + 1)], axis=0
            )
            for d in range(1, 8):
                total += rbuf[h, gpeer(d), i * 8 : i * 8 + 16].astype(F32)
            factor += [total[0:8], total[8:16]]
        coefs = kft[pl.ds(pl.multiple_of(64 * h + 8 * g, 8), 8)]
        results = {}
        for j in range(2):
            abs_z = (2 * k + j).astype(F32)
            mag = jnp.sqrt(abs_x * abs_x + abs_y * abs_y + abs_z * abs_z) * (2.0 * math.pi / 8.0)
            radial = (mag - kappa) * (KQ / 21.0)
            radial = jnp.exp(radial * radial * -0.5)
            kfilt = jnp.zeros((8, 128), F32)
            for p in range(KQ):
                kfilt += coefs[:, p : p + 1] * radial[p : p + 1]
            kfilt = kfilt * float(ATOMS * KW) ** -0.5
            names = ((0, 0, 0), (1, 0, 1), (1, 1, 0), (0, 1, 1), (0, 1, 0), (0, 0, 1), (1, 0, 0), (1, 1, 1))
            values = [
                factor[tz * 2 + j][:, (tx * 2 + ty) * 128 : (tx * 2 + ty + 1) * 128] for tz, tx, ty in names
            ]
            even, odd = values[:4], values[4:]
            out_even = [0.0] * 4
            out_odd = [0.0] * 4
            for cl in range(4):
                pxy, pxz = 1.0 - 2.0 * (cl // 2), 1.0 - 2.0 * (cl % 2)
                pyz = pxy * pxz
                weight = pres[cl * 2 + j : cl * 2 + j + 1] * kfilt
                for parts, out, signs in (
                    (even, out_even, (1.0, -pyz, -pxz, -pxy)),
                    (odd, out_odd, (1.0, pxy, pxz, -pyz)),
                ):
                    value = parts[0]
                    for s, p in zip(signs[1:], parts[1:]):
                        value = value + p if s > 0 else value - p
                    value = value * weight
                    for i in range(4):
                        out[i] = out[i] + value if signs[i] > 0 else out[i] - value
            for (tz, tx, ty), value in zip(names, out_even + out_odd):
                results[tz, j, tx, ty] = value
        for tz in range(2):
            for tx in range(2):
                for ty in range(2):
                    at = (tx * 2 + ty) * 128
                    both = jnp.concatenate([results[tz, 0, tx, ty], results[tz, 1, tx, ty]], axis=0)
                    gbuf[h, g, tz * 16 : tz * 16 + 16, at : at + 128] = both.astype(BF16)
        for d in (6, 2, 5, 7, 1, 3, 4):
            ag_copy(h, d, g).start()

    def ag_copy(h, d, slot):
        r = gbuf.at[h, slot]
        return send(r, r, a_s.at[h, d], a_r.at[h, slot], (gpeer(d) * 2 + core, k))

    eye = jnp.where(
        lax.broadcasted_iota(jnp.int32, (128, 128), 0) == lax.broadcasted_iota(jnp.int32, (128, 128), 1), 1.0, 0.0
    )

    def pair_step(b):
        me = jnp.transpose(window[own + b, 0:16].astype(F32))
        mx, my, mz = (me[:, i : i + 1] + me[:, i + 3 : i + 4] + me[:, i + 6 : i + 7] for i in range(3))
        my_block = a * 16 + 2 * k + b

        def one(n):
            ident = nb_ref[b, n]
            at = jnp.clip((ident - (2 * g - 1) * 16 + 256) % 256, 0, 63)
            r = window[at, 0:16].astype(F32)
            px, py, pz = (r[i : i + 1] + r[i + 3 : i + 4] + r[i + 6 : i + 7] for i in range(3))
            same = jnp.where(ident == my_block, 1.0, 0.0)
            dx, dy, dz = mx - px, my - py, mz - pz
            d2 = dx * dx + dy * dy + dz * dz
            u = d2 * lax.rsqrt(jnp.maximum(d2, 1e-30)) * (8.0 / 12.0)
            env = (1.0 - eye * same) * float(NS * BLK) ** -0.5 / (1.0 + d2 * (1.0 / 16.0))
            v = u - 0.5
            level = jnp.exp(v * v * -0.5) * env
            ratio = jnp.exp(u - 4.0)
            cols = slice(n * 128, (n + 1) * 128)
            for i in range(KB):
                basis[i * 128 : (i + 1) * 128, cols] = level.astype(BF16)
                if i < KB - 1:
                    level = level * ratio
            near[:, cols] = window[at, 16:144]

        def product(p):
            cols = slice(p * 256, (p + 1) * 256)
            return lax.dot_general(basis[:, cols], near[:, cols], NT, preferred_element_type=F32)

        sums = 0.0
        for p in range(NS // 2):
            one(2 * p)
            one(2 * p + 1)
            if p:
                sums = sums + product(p - 1)
        sums = sums + product(NS // 2 - 1)
        for i in range(KB):
            scale = math.exp(4.0 * i - 0.5 * i * (i + 1))
            summed[:, i * 128 : (i + 1) * 128] = (sums[i * 128 : (i + 1) * 128] * scale).astype(BF16)
        pair[b * 128 : (b + 1) * 128] = jnp.dot(summed[...], pw_ref[...], preferred_element_type=F32)

    filter_half(0)
    spread(4, ky).wait_recv()
    for d in (1, 3, 2):
        spread(d, ky).start()
    filter_half(1)
    for load in loads[5:7]:
        load.wait()

    def sib_part(h, kk):
        return send(sibs.at[h, kk], sibin.at[h, kk], b_s.at[h, kk], b_r.at[h, kk], sib)

    def own_part(h, d, src, slot):
        return send(lsend.at[h, src], lbuf.at[h, slot], l_s.at[h, d], l_r.at[h, slot], (a, kpeer(d)))

    def message(h, kk):
        values = jnp.dot(gbuf[h].reshape(256, 512), tabs[kk], preferred_element_type=F32)
        fz = [ztab[kk, i : i + 1] for i in range(4)]
        for t in range(0, 8, 2):
            pieces = []
            for u in (t, t + 1):
                total = values[u * 32 : u * 32 + 8] * fz[0]
                for i in range(1, 4):
                    total += values[u * 32 + i * 8 : u * 32 + (i + 1) * 8] * fz[i]
                pieces.append(total)
            both = jnp.concatenate(pieces, axis=0)
            low, high = both[:, 0:256], both[:, 256:512]
            lown[h, kk, t * 8 : t * 8 + 16] = jnp.where(core == 0, low, high)
            sibs[h, kk, t * 8 : t * 8 + 16] = jnp.where(core == 0, high, low).astype(BF16)
        sib_part(h, kk).start()

    def passed_on(h, d):
        kk = kpeer(d)
        sib_part(h, kk).wait_recv()
        lsend[h, kk] = (lown[h, kk] + sibin[h, kk].astype(F32)).astype(BF16)
        own_part(h, d, kk, k).start()

    for h in range(2):
        for d in range(1, 8):
            ag_copy(h, d, gpeer(d)).wait_recv()
        message(h, kpeer(7))
        message(h, kpeer(6))

        def message_loop(i, carry):
            message(h, kpeer(7 - i))
            passed_on(h, 9 - i)
            return carry

        lax.fori_loop(2, 7, message_loop, 0)
        message(h, k)
        passed_on(h, 2)
        passed_on(h, 1)

    for d in (1, 2, 3, 5, 6, 7):
        spread(d, kpeer(d)).wait_recv()
    pair_step(0)
    pair_step(1)
    rest = feat_ref[...].astype(F32) + pair[...]
    for load in loads[7:]:
        load.wait()
    longs = []
    for h in range(2):
        sib_part(h, k).wait_recv()
        long = lown[h, k] + sibin[h, k].astype(F32)
        for d in range(1, 8):
            own_part(h, d, kpeer(d), kpeer(d)).wait_recv()
            long += lbuf[h, kpeer(d)].astype(F32)
        longs.append(long)

    total = rest + jnp.transpose(jnp.concatenate(longs, axis=0))
    mean = jnp.mean(total * total, axis=-1, keepdims=True)
    normed = (total * lax.rsqrt(mean + 1e-6) * gain_ref[...]).astype(BF16)
    hidden = jnp.dot(normed, win_ref[...], preferred_element_type=F32)
    hidden = (hidden / (1.0 + jnp.exp(-hidden))).astype(BF16)
    out_ref[...] = (total + jnp.dot(hidden, wout_ref[...], preferred_element_type=F32)).astype(BF16)

    halo_copy(own, at_halo(other, k)).wait_send()
    for h in range(2):
        sib_copy(h, core, k).wait_send()
        sib_part(h, k).wait_send()
        for d in range(1, 8):
            kk = kpeer(d)
            group_copy(h, d, k).wait_send()
            sib_copy(h, core, kk).wait_send()
            rs_copy(h, d, gpeer(d), g).wait_send()
            ag_copy(h, d, g).wait_send()
            sib_part(h, kk).wait_send()
            own_part(h, d, kk, k).wait_send()
    spread(4, k).wait_send()
    for d in range(1, 4):
        spread(d, k).wait_send()
        spread(d, ky).wait_send()


def per_device(positions, features, atom_mask, neighbours, lattice, pair_weight, kfilter, norm_gain, w_in, w_out):
    dma = pltpu.SemaphoreType.DMA((2, 8))
    operands = (
        positions, features, atom_mask.reshape(1, -1), neighbours, lattice, pair_weight, kfilter,
        norm_gain.reshape(1, -1), w_in, w_out,
    )
    return pl.pallas_call(
        kernel,
        out_shape=jax.ShapeDtypeStruct(features.shape, BF16),
        in_specs=[pl.BlockSpec(memory_space=pl.ANY)] * len(operands),
        out_specs=pl.BlockSpec(memory_space=pltpu.VMEM),
        scratch_shapes=[
            (pltpu.SMEM if x is neighbours else pltpu.VMEM)(x.shape, x.dtype) for x in operands
        ]
        + [
            pltpu.SemaphoreType.DMA((10,)),
            pltpu.VMEM((64, 144, 128), BF16),
            pltpu.VMEM((2, 16, 128), F32),
            pltpu.VMEM((8, 512, 512), BF16),
            pltpu.VMEM((8, 8, 512), F32),
            pltpu.VMEM((256, 512), BF16),
            pltpu.VMEM((2, 256, 512), F32),
            pltpu.VMEM((16, 128), F32),
            pltpu.VMEM((128, 8), F32),
            pltpu.VMEM((2, 8, 32, 512), BF16),
            pltpu.VMEM((2, 8, 32, 512), BF16),
            pltpu.VMEM((2, 8, 32, 512), BF16),
            pltpu.VMEM((2, 8, 64, 256), F32),
            pltpu.VMEM((2, 8, 64, 256), BF16),
            pltpu.VMEM((2, 8, 64, 256), BF16),
            pltpu.VMEM((2, 8, 64, 256), BF16),
            pltpu.VMEM((2, 8, 64, 256), BF16),
            pltpu.VMEM((1024, 1536), BF16),
            pltpu.VMEM((128, 1536), BF16),
            pltpu.VMEM((128, 1024), BF16),
            pltpu.VMEM((256, 128), F32),
        ]
        + [dma] * 4
        + [pltpu.SemaphoreType.DMA((1,))] * 2
        + [pltpu.SemaphoreType.DMA((8,))] * 2
        + [dma] * 8,
        compiler_params=pltpu.CompilerParams(
            collective_id=0, has_side_effects=True, vmem_limit_bytes=56 * 1024 * 1024
        ),
    )(*operands)


def solution(mesh):
    return jax.shard_map(
        per_device,
        mesh=mesh,
        in_specs=(
            P(None, ("atoms", "kvec")),
            P(("atoms", "kvec"), None),
            P(("atoms", "kvec")),
            P(("atoms", "kvec"), None),
            P(None, "kvec"),
            P(),
            P(),
            P(),
            P(),
            P(),
        ),
        out_specs=P(("atoms", "kvec"), None),
        check_vma=False,
    )
```

```python
import math

import jax
import jax.numpy as jnp
from jax import lax
from jax.experimental import pallas as pl
from jax.experimental.pallas import tpu as pltpu
from jax.sharding import PartitionSpec as P

MESH = pl.DeviceIdType.MESH
F32 = jnp.float32
BF16 = jnp.bfloat16
KW = 12288
BLK = 128
C = 128
KB = 8
KQ = 8
NS = 12
ATOMS = 32768
NT = (((1,), (1,)), ((), ()))

SIN = tuple((-1.0) ** i / math.factorial(2 * i + 1) for i in range(6))
COS = tuple((-1.0) ** i / math.factorial(2 * i) for i in range(7))


def poly(h2, coefs):
    total = h2 * coefs[-1] + coefs[-2]
    for c in coefs[-3::-1]:
        total = total * h2 + c
    return total


def sincos_turns(turns):
    h = (turns - jnp.floor(turns + 0.5)) * math.pi
    h2 = h * h
    s = h * poly(h2, SIN)
    c = poly(h2, COS)
    return 2.0 * s * c, 1.0 - 2.0 * s * s


def kernel(
    pos_in, feat_in, mask_in, nb_in, lat_in, pw_in, kfilter_in, gain_in, win_in, wout_in,
    out_ref,
    pos_ref, feat_ref, mask_ref, nb_ref, lat_ref, pw_ref, kfilter_ref, gain_ref, win_ref, wout_ref, in_sem,
    window, stage, tabs, ztab, zm, acc, pres, kft, pbuf, rbuf, gbuf, lown, sibs, sibin, lsend, lbuf,
    basis, near, summed, pair,
    g_s, g_r, s_s, s_r, h_s, h_r, x_s, x_r, r_s, r_r, a_s, a_r, b_s, b_r, l_s, l_r,
):
    a = lax.axis_index("atoms")
    k = lax.axis_index("kvec")
    core = lax.rem(a, 2)
    g = a // 2
    other = 1 - core
    sib = (g * 2 + other, k)

    def kpeer(d):
        return ((k // 4 + d // 4) % 2) * 4 + (k % 4 + d % 4) % 4

    def gpeer(d):
        return ((g // 4 + d // 4) % 2) * 4 + (g % 4 + d % 4) % 4

    halo_dev = (((g + jnp.where(core == 1, 1, 7)) % 8) * 2 + other, k)

    loads = [
        pltpu.make_async_copy(src, dst, in_sem.at[i])
        for i, (src, dst) in enumerate((
            (lat_in, lat_ref), (feat_in, feat_ref), (mask_in, mask_ref), (pos_in, pos_ref), (kfilter_in, kfilter_ref),
            (nb_in, nb_ref), (pw_in, pw_ref), (gain_in, gain_ref), (win_in, win_ref), (wout_in, wout_ref),
        ))
    ]
    barrier = pltpu.get_barrier_semaphore()
    for d in range(1, 8):
        pl.semaphore_signal(barrier, inc=1, device_id=(gpeer(d) * 2 + core, k), device_id_type=MESH)
        pl.semaphore_signal(barrier, inc=1, device_id=(a, kpeer(d)), device_id_type=MESH)
    pl.semaphore_signal(barrier, inc=1, device_id=halo_dev, device_id_type=MESH)
    pl.semaphore_signal(barrier, inc=1, device_id=sib, device_id_type=MESH)
    for load in loads:
        load.start()

    def at_core(c, kk):
        return 16 + c * 16 + 2 * kk

    def at_halo(c, kk):
        return c * 48 + 2 * kk

    own = at_core(core, k)
    acc[...] = jnp.zeros_like(acc)
    pres[...] = jnp.zeros_like(pres)
    for load in loads[:5]:
        load.wait()
    lat = lat_ref[:, pl.ds(pl.multiple_of(core * 768, 128), 768)]
    nx, ny, nz = lat[0:1], lat[1:2], lat[2:3]
    bx, by, bz = (jnp.where(n < 0, 1, 0) for n in (nx, ny, nz))
    cls = jnp.where(bx != by, 2, 0) + jnp.where(bx != bz, 1, 0)
    code_xy = (jnp.abs(nx) * 16 + jnp.abs(ny)).astype(F32)
    code_z = (cls * 16 + jnp.abs(nz)).astype(F32)
    masked = jnp.transpose(feat_ref[...].astype(F32)) * mask_ref[...].astype(F32)
    stage[...] = jnp.zeros_like(stage)
    for b in range(2):
        rest = pos_ref[:, b * 128 : (b + 1) * 128]
        for i in range(3):
            piece = rest.astype(BF16).astype(F32)
            stage[b, 3 * i : 3 * i + 3] = piece
            rest = rest - piece
        for r in range(3):
            at = (b * 3 + r) * 128
            stage[b, 9 + r : 10 + r] = code_xy[:, at : at + 128]
            stage[b, 12 + r : 13 + r] = code_z[:, at : at + 128]
        window[own + b, 0:16] = stage[b].astype(BF16)
        window[own + b, 16:144] = masked[:, b * 128 : (b + 1) * 128].astype(BF16)
    kft[...] = jnp.transpose(kfilter_ref[...])
    pl.semaphore_wait(barrier, 16)

    def half(at, h):
        return window.at[pl.ds(at, 2), pl.ds(80 * h, 80 - 16 * h)]

    def send(src, dst, ss, rs, dev):
        return pltpu.make_async_remote_copy(
            src_ref=src, dst_ref=dst, send_sem=ss, recv_sem=rs, device_id=dev, device_id_type=MESH
        )

    def group_copy(h, d, kk):
        r = half(at_core(core, kk), h)
        return send(r, r, g_s.at[h, d], g_r.at[h, kk], (a, kpeer(d)))

    def sib_copy(h, c, kk):
        r = half(at_core(c, kk), h)
        return send(r, r, s_s.at[h, kk], s_r.at[h, kk], sib)

    def halo_copy(src, dst):
        return send(window.at[pl.ds(src, 2)], window.at[pl.ds(dst, 2)], h_s.at[0], h_r.at[0], halo_dev)

    ky = (k + 4) % 8

    def spread(d, kk):
        r = window.at[pl.ds(at_halo(core, kk), 2)]
        at = d - 1 if kk is k else d + 3
        return send(r, r, x_s.at[at], x_r.at[kk], (a, kpeer(d)))

    sib_copy(0, core, k).start()
    for d in range(1, 8):
        group_copy(0, d, k).start()
    halo_copy(own, at_halo(other, k)).start()
    sib_copy(1, core, k).start()

    def row_numbers(rows):
        return lax.broadcasted_iota(jnp.int32, (rows, 512), 0)

    numbers = jnp.concatenate(
        [row_numbers(16), row_numbers(8) + 8 * core, 2 * k + lax.rem(row_numbers(8), 2)], axis=0
    ).astype(F32) * 0.125

    def joined(kk, low, count):
        return jnp.concatenate(
            [window[at_core(c, kk) + b, low : low + count] for c in range(2) for b in range(2)], axis=1
        ).astype(F32)

    def tables(kk):
        rows = joined(kk, 0, 16)
        px, py, pz = (rows[i : i + 1] + rows[i + 3 : i + 4] + rows[i + 6 : i + 7] for i in range(3))
        coord = jnp.concatenate(
            [jnp.broadcast_to(py, (16, 512)), jnp.broadcast_to(px, (8, 512)), jnp.broadcast_to(pz, (8, 512))],
            axis=0,
        )
        sines, cosines = sincos_turns(coord * numbers)
        fy = (cosines[0:16], sines[0:16])
        for tx, fx in enumerate((cosines[16:24], sines[16:24])):
            for ix in range(8):
                row = fx[ix : ix + 1]
                for ty in range(2):
                    at = ((tx * 2 + ty) * 8 + ix) * 16
                    tabs[kk, at : at + 16] = (row * fy[ty]).astype(BF16)
        for i, row in enumerate((cosines[24:25], cosines[25:26], sines[24:25], sines[25:26])):
            ztab[kk, i : i + 1] = row

    def factor_step(h, kk):
        rows = joined(kk, 16 + 64 * h, 64)
        for i in range(4):
            zm[i * 64 : (i + 1) * 64] = (rows * ztab[kk, i : i + 1]).astype(BF16)
        acc[h] += lax.dot_general(zm[...], tabs[kk], NT, preferred_element_type=F32)

    def arrive(h, d):
        kk = kpeer(d)
        group_copy(h, 0, kk).wait_recv()
        sib_copy(h, core, kk).start()
        if h == 0:
            group_copy(1, d, k).start()

    def use(h, kk):
        sib_copy(h, other, kk).wait_recv()
        if h == 0:
            tables(kk)
        factor_step(h, kk)

    def rs_copy(h, d, src, slot):
        return send(pbuf.at[h, src], rbuf.at[h, slot], r_s.at[h, d], r_r.at[h, slot], (gpeer(d) * 2 + core, k))

    def gather_half(h):
        arrive(h, 1)

        def step(d, carry):
            arrive(h, d)
            use(h, kpeer(d - 2))
            return carry

        lax.fori_loop(2, 8, step, 0)
        use(h, kpeer(6))
        use(h, kpeer(7))
        for d in (6, 2, 5, 7, 1, 3, 4):
            t = gpeer(d)
            for i in range(0, 4, 2):
                rows = jnp.concatenate(
                    [acc[h, pl.ds(pl.multiple_of(j * 64 + 8 * t, 8), 8)] for j in (i, i + 1)], axis=0
                )
                pbuf[h, t, i * 8 : i * 8 + 16] = rows.astype(BF16)
            rs_copy(h, d, t, g).start()

    gather_half(0)
    gather_half(1)


    xy_rows = lax.broadcasted_iota(jnp.int32, (128, 512), 0) + 128 * core
    zr = lax.broadcasted_iota(jnp.int32, (16, 512), 0)
    z_rows = ((zr // 2) * 16 + 2 * k + lax.rem(zr, 2)).astype(F32)
    xy_rows = xy_rows.astype(F32)

    def presence_step(kk, carry):
        rows = joined(kk, 0, 16)
        for r in range(3):
            hot_xy = jnp.where(rows[9 + r : 10 + r] == xy_rows, 1.0, 0.0).astype(BF16)
            hot_z = jnp.where(rows[12 + r : 13 + r] == z_rows, 1.0, 0.0).astype(BF16)
            pres[...] += lax.dot_general(hot_z, hot_xy, NT, preferred_element_type=F32)
        return carry

    lax.fori_loop(0, 8, presence_step, 0)

    lane = lax.broadcasted_iota(jnp.int32, (8, 128), 1)
    abs_x = (lane // 16 + 8 * core).astype(F32)
    abs_y = lax.rem(lane, 16).astype(F32)
    kappa = (lax.broadcasted_iota(jnp.int32, (8, 128), 0).astype(F32) + 0.5) * (21.0 / KQ)

    def filter_half(h):
        for d in range(1, 8):
            rs_copy(h, d, gpeer(d), gpeer(d)).wait_recv()
        factor = []
        for i in range(0, 4, 2):
            total = jnp.concatenate(
                [acc[h, pl.ds(pl.multiple_of(j * 64 + 8 * g, 8), 8)] for j in (i, i + 1)], axis=0
            )
            for d in range(1, 8):
                total += rbuf[h, gpeer(d), i * 8 : i * 8 + 16].astype(F32)
            factor += [total[0:8], total[8:16]]
        coefs = kft[pl.ds(pl.multiple_of(64 * h + 8 * g, 8), 8)]
        results = {}
        for j in range(2):
            abs_z = (2 * k + j).astype(F32)
            mag = jnp.sqrt(abs_x * abs_x + abs_y * abs_y + abs_z * abs_z) * (2.0 * math.pi / 8.0)
            radial = (mag - kappa) * (KQ / 21.0)
            radial = jnp.exp(radial * radial * -0.5)
            kfilt = jnp.zeros((8, 128), F32)
            for p in range(KQ):
                kfilt += coefs[:, p : p + 1] * radial[p : p + 1]
            kfilt = kfilt * float(ATOMS * KW) ** -0.5
            names = ((0, 0, 0), (1, 0, 1), (1, 1, 0), (0, 1, 1), (0, 1, 0), (0, 0, 1), (1, 0, 0), (1, 1, 1))
            values = [
                factor[tz * 2 + j][:, (tx * 2 + ty) * 128 : (tx * 2 + ty + 1) * 128] for tz, tx, ty in names
            ]
            even, odd = values[:4], values[4:]
            out_even = [0.0] * 4
            out_odd = [0.0] * 4
            for cl in range(4):
                pxy, pxz = 1.0 - 2.0 * (cl // 2), 1.0 - 2.0 * (cl % 2)
                pyz = pxy * pxz
                weight = pres[cl * 2 + j : cl * 2 + j + 1] * kfilt
                for parts, out, signs in (
                    (even, out_even, (1.0, -pyz, -pxz, -pxy)),
                    (odd, out_odd, (1.0, pxy, pxz, -pyz)),
                ):
                    value = parts[0]
                    for s, p in zip(signs[1:], parts[1:]):
                        value = value + p if s > 0 else value - p
                    value = value * weight
                    for i in range(4):
                        out[i] = out[i] + value if signs[i] > 0 else out[i] - value
            for (tz, tx, ty), value in zip(names, out_even + out_odd):
                results[tz, j, tx, ty] = value
        for tz in range(2):
            for tx in range(2):
                for ty in range(2):
                    at = (tx * 2 + ty) * 128
                    both = jnp.concatenate([results[tz, 0, tx, ty], results[tz, 1, tx, ty]], axis=0)
                    gbuf[h, g, tz * 16 : tz * 16 + 16, at : at + 128] = both.astype(BF16)
        for d in (6, 2, 5, 7, 1, 3, 4):
            ag_copy(h, d, g).start()

    def ag_copy(h, d, slot):
        r = gbuf.at[h, slot]
        return send(r, r, a_s.at[h, d], a_r.at[h, slot], (gpeer(d) * 2 + core, k))

    eye = jnp.where(
        lax.broadcasted_iota(jnp.int32, (128, 128), 0) == lax.broadcasted_iota(jnp.int32, (128, 128), 1), 1.0, 0.0
    )

    def pair_step(b):
        me = jnp.transpose(window[own + b, 0:16].astype(F32))
        mx, my, mz = (me[:, i : i + 1] + me[:, i + 3 : i + 4] + me[:, i + 6 : i + 7] for i in range(3))
        my_block = a * 16 + 2 * k + b

        def one(n):
            ident = nb_ref[b, n]
            at = jnp.clip((ident - (2 * g - 1) * 16 + 256) % 256, 0, 63)
            r = window[at, 0:16].astype(F32)
            px, py, pz = (r[i : i + 1] + r[i + 3 : i + 4] + r[i + 6 : i + 7] for i in range(3))
            same = jnp.where(ident == my_block, 1.0, 0.0)
            dx, dy, dz = mx - px, my - py, mz - pz
            d2 = dx * dx + dy * dy + dz * dz
            u = d2 * lax.rsqrt(jnp.maximum(d2, 1e-30)) * (8.0 / 12.0)
            env = (1.0 - eye * same) * float(NS * BLK) ** -0.5 / (1.0 + d2 * (1.0 / 16.0))
            v = u - 0.5
            level = jnp.exp(v * v * -0.5) * env
            ratio = jnp.exp(u - 4.0)
            cols = slice(n * 128, (n + 1) * 128)
            for i in range(KB):
                basis[i * 128 : (i + 1) * 128, cols] = level.astype(BF16)
                if i < KB - 1:
                    level = level * ratio
            near[:, cols] = window[at, 16:144]

        def product(p):
            cols = slice(p * 256, (p + 1) * 256)
            return lax.dot_general(basis[:, cols], near[:, cols], NT, preferred_element_type=F32)

        sums = 0.0
        for p in range(NS // 2):
            one(2 * p)
            one(2 * p + 1)
            if p:
                sums = sums + product(p - 1)
        sums = sums + product(NS // 2 - 1)
        for i in range(KB):
            scale = math.exp(4.0 * i - 0.5 * i * (i + 1))
            summed[:, i * 128 : (i + 1) * 128] = (sums[i * 128 : (i + 1) * 128] * scale).astype(BF16)
        pair[b * 128 : (b + 1) * 128] = jnp.dot(summed[...], pw_ref[...], preferred_element_type=F32)

    filter_half(0)
    halo_copy(own, at_halo(core, k)).wait_recv()
    for d in (4, 1, 3, 2):
        spread(d, k).start()
    filter_half(1)
    spread(4, ky).wait_recv()
    for d in (1, 3, 2):
        spread(d, ky).start()
    for load in loads[5:7]:
        load.wait()

    def sib_part(h, kk):
        return send(sibs.at[h, kk], sibin.at[h, kk], b_s.at[h, kk], b_r.at[h, kk], sib)

    def own_part(h, d, src, slot):
        return send(lsend.at[h, src], lbuf.at[h, slot], l_s.at[h, d], l_r.at[h, slot], (a, kpeer(d)))

    def message(h, kk):
        values = jnp.dot(gbuf[h].reshape(256, 512), tabs[kk], preferred_element_type=F32)
        fz = [ztab[kk, i : i + 1] for i in range(4)]
        for t in range(0, 8, 2):
            pieces = []
            for u in (t, t + 1):
                total = values[u * 32 : u * 32 + 8] * fz[0]
                for i in range(1, 4):
                    total += values[u * 32 + i * 8 : u * 32 + (i + 1) * 8] * fz[i]
                pieces.append(total)
            both = jnp.concatenate(pieces, axis=0)
            low, high = both[:, 0:256], both[:, 256:512]
            lown[h, kk, t * 8 : t * 8 + 16] = jnp.where(core == 0, low, high)
            sibs[h, kk, t * 8 : t * 8 + 16] = jnp.where(core == 0, high, low).astype(BF16)
        sib_part(h, kk).start()

    def passed_on(h, d):
        kk = kpeer(d)
        sib_part(h, kk).wait_recv()
        lsend[h, kk] = (lown[h, kk] + sibin[h, kk].astype(F32)).astype(BF16)
        own_part(h, d, kk, k).start()

    for h in range(2):
        for d in range(1, 8):
            ag_copy(h, d, gpeer(d)).wait_recv()
        message(h, kpeer(7))
        message(h, kpeer(6))
        message(h, kpeer(5))

        def message_loop(i, carry):
            message(h, kpeer(7 - i))
            passed_on(h, 10 - i)
            return carry

        lax.fori_loop(3, 7, message_loop, 0)
        passed_on(h, 3)
        passed_on(h, 2)
        message(h, k)
        passed_on(h, 1)

    for d in (1, 2, 3, 5, 6, 7):
        spread(d, kpeer(d)).wait_recv()
    pair_step(0)
    pair_step(1)
    rest = feat_ref[...].astype(F32) + pair[...]
    for load in loads[7:]:
        load.wait()
    longs = []
    for h in range(2):
        sib_part(h, k).wait_recv()
        long = lown[h, k] + sibin[h, k].astype(F32)
        for d in range(1, 8):
            own_part(h, d, kpeer(d), kpeer(d)).wait_recv()
            long += lbuf[h, kpeer(d)].astype(F32)
        longs.append(long)

    total = rest + jnp.transpose(jnp.concatenate(longs, axis=0))
    mean = jnp.mean(total * total, axis=-1, keepdims=True)
    normed = (total * lax.rsqrt(mean + 1e-6) * gain_ref[...]).astype(BF16)
    hidden = jnp.dot(normed, win_ref[...], preferred_element_type=F32)
    hidden = (hidden / (1.0 + jnp.exp(-hidden))).astype(BF16)
    out_ref[...] = (total + jnp.dot(hidden, wout_ref[...], preferred_element_type=F32)).astype(BF16)

    halo_copy(own, at_halo(other, k)).wait_send()
    for h in range(2):
        sib_copy(h, core, k).wait_send()
        sib_part(h, k).wait_send()
        for d in range(1, 8):
            kk = kpeer(d)
            group_copy(h, d, k).wait_send()
            sib_copy(h, core, kk).wait_send()
            rs_copy(h, d, gpeer(d), g).wait_send()
            ag_copy(h, d, g).wait_send()
            sib_part(h, kk).wait_send()
            own_part(h, d, kk, k).wait_send()
    spread(4, k).wait_send()
    for d in range(1, 4):
        spread(d, k).wait_send()
        spread(d, ky).wait_send()


def per_device(positions, features, atom_mask, neighbours, lattice, pair_weight, kfilter, norm_gain, w_in, w_out):
    dma = pltpu.SemaphoreType.DMA((2, 8))
    operands = (
        positions, features, atom_mask.reshape(1, -1), neighbours, lattice, pair_weight, kfilter,
        norm_gain.reshape(1, -1), w_in, w_out,
    )
    return pl.pallas_call(
        kernel,
        out_shape=jax.ShapeDtypeStruct(features.shape, BF16),
        in_specs=[pl.BlockSpec(memory_space=pl.ANY)] * len(operands),
        out_specs=pl.BlockSpec(memory_space=pltpu.VMEM),
        scratch_shapes=[
            (pltpu.SMEM if x is neighbours else pltpu.VMEM)(x.shape, x.dtype) for x in operands
        ]
        + [
            pltpu.SemaphoreType.DMA((10,)),
            pltpu.VMEM((64, 144, 128), BF16),
            pltpu.VMEM((2, 16, 128), F32),
            pltpu.VMEM((8, 512, 512), BF16),
            pltpu.VMEM((8, 8, 512), F32),
            pltpu.VMEM((256, 512), BF16),
            pltpu.VMEM((2, 256, 512), F32),
            pltpu.VMEM((16, 128), F32),
            pltpu.VMEM((128, 8), F32),
            pltpu.VMEM((2, 8, 32, 512), BF16),
            pltpu.VMEM((2, 8, 32, 512), BF16),
            pltpu.VMEM((2, 8, 32, 512), BF16),
            pltpu.VMEM((2, 8, 64, 256), F32),
            pltpu.VMEM((2, 8, 64, 256), BF16),
            pltpu.VMEM((2, 8, 64, 256), BF16),
            pltpu.VMEM((2, 8, 64, 256), BF16),
            pltpu.VMEM((2, 8, 64, 256), BF16),
            pltpu.VMEM((1024, 1536), BF16),
            pltpu.VMEM((128, 1536), BF16),
            pltpu.VMEM((128, 1024), BF16),
            pltpu.VMEM((256, 128), F32),
        ]
        + [dma] * 4
        + [pltpu.SemaphoreType.DMA((1,))] * 2
        + [pltpu.SemaphoreType.DMA((8,))] * 2
        + [dma] * 8,
        compiler_params=pltpu.CompilerParams(
            collective_id=0, has_side_effects=True, vmem_limit_bytes=56 * 1024 * 1024
        ),
    )(*operands)


def solution(mesh):
    return jax.shard_map(
        per_device,
        mesh=mesh,
        in_specs=(
            P(None, ("atoms", "kvec")),
            P(("atoms", "kvec"), None),
            P(("atoms", "kvec")),
            P(("atoms", "kvec"), None),
            P(None, "kvec"),
            P(),
            P(),
            P(),
            P(),
            P(),
        ),
        out_specs=P(("atoms", "kvec"), None),
        check_vma=False,
    )
```
